32 devices in a mesh: sub: 4 (over x, core), front: 8 (over z, y).
Axes of the slice: x: 2, y: 2, z: 4, core: 2. Of those that a mesh axis runs over, the one named last changes fastest.
Arguments:
- factor_inverse: bfloat16 [4, 2, 4096, 4096], P('sub', None, 'front'), as said below
- contribution: bfloat16 [4, 2, 4096, 4096], P('sub', None, None, 'front'), may hold values from -0.09375 to 0.09375
- block_map: int32 [4, 2, 32], P('sub'), may hold values from 0 to 31, as said below
- sep_size: int32 [4, 2], P('sub'), may hold values from 1024 to 4096, as said below
- right_side: float32 [4, 2, 4096, 128], P('sub', None, 'front'), may hold values from -6 to 6
Outputs:
- solution: float32 [4, 2, 4096, 128], P('sub', None, 'front')
The draws below stay inside these ranges and needn't reach their ends.
Inputs may be any that keep to these rules, and one draw needn't show every extreme that they name: `block_map`: for each front the 32 entries are all different. `sep_size`: front (0, 1) always uses all 4096 rows, leaf 4 - 1 uses 4096 // 4. `factor_inverse`: every block is zero above its diagonal.
All inputs are finite; a program needn't handle non-finite values.
Results may differ from the reference program's by a relative error of at most 0.023.
Values may be sent and summed in bfloat16 or wider, within the bound.
A program may use at most 192 MiB of HBM per device.

```python
import math
import jax
import jax.numpy as jnp

SEP = 4096
NRHS = 128
BLK = 128
BLOCKS = 32
N_SUB = 4


def draw_factor_inverse(key, part):
    key = jax.random.fold_in(key, 11)
    key_off, key_diag = jax.random.split(key)
    shape = (N_SUB, 2, SEP, SEP)
    offdiag = jax.random.normal(key_off, shape, jnp.float32) * (0.7 / math.sqrt(SEP))
    diagonal = jnp.exp(jax.random.uniform(key_diag, (N_SUB, 2, SEP, 1), jnp.float32, 0.0, math.log(2.5)))
    row_ids = jnp.arange(SEP, dtype=jnp.int32)[:, None]
    col_ids = jnp.arange(SEP, dtype=jnp.int32)[None, :]
    lower = jnp.where(col_ids < row_ids, offdiag, 0.0)
    return (lower + jnp.where(col_ids == row_ids, diagonal, 0.0)).astype(jnp.bfloat16)


def draw_block_map(key, part):
    key = jax.random.fold_in(key, 23)
    keys = jax.random.split(key, N_SUB * 2)
    orders = jax.vmap(lambda single: jax.random.permutation(single, BLOCKS))(keys)
    return orders.reshape(N_SUB, 2, BLOCKS).astype(jnp.int32)


def draw_sep_size(key, part):
    key = jax.random.fold_in(key, 37)
    sizes = jax.random.randint(key, (N_SUB, 2), SEP // 4, SEP + 1).astype(jnp.int32)
    sizes = sizes.at[0, 1].set(SEP)
    return sizes.at[N_SUB - 1, 0].set(SEP // 4)


def block_levels(own_key, dims, pieces, low, largest):
    gain = 1.0
    for position, parts in pieces:
        draws = jax.random.uniform(jax.random.fold_in(jax.random.fold_in(own_key, 6), position), (parts,), jnp.float32, low / len(pieces), largest / len(pieces))
        gain = gain * jnp.repeat(jnp.exp(draws), dims[position] // parts).reshape((-1,) + (1,) * (len(dims) - 1 - position))
    return gain


def scatter_about(rng, shape, width, most, shards=(), held_as=jnp.bfloat16):
    result = jax.random.normal(rng, shape, jnp.float32) * width
    if len(shards) > 0:
        result = block_levels(rng, shape, shards, -0.22, 0.18) * result
    return jnp.clip(result, min=-most, max=most).astype(held_as)


def setup_inputs(seed: int = 0) -> dict:
    splits = jax.random.split(jax.random.key(seed), 6)
    factor_inverse = draw_factor_inverse(jax.random.fold_in(splits[5], 71), 0)
    contribution = scatter_about(splits[1], (N_SUB, 2, SEP, SEP), SEP ** -0.5, 0.09375, ((0, 4), (3, 8)))
    block_map = draw_block_map(jax.random.fold_in(splits[5], 71), 0)
    sep_size = draw_sep_size(jax.random.fold_in(splits[5], 71), 0)
    right_side = scatter_about(splits[4], (N_SUB, 2, SEP, NRHS), 1.0, 6.0, ((0, 4), (2, 8)), jnp.float32)
    return dict(factor_inverse=factor_inverse, contribution=contribution, block_map=block_map, sep_size=sep_size, right_side=right_side)


def front_height(group, top):
    if group == 0:
        return top + 1
    height = 1
    while group % 2 == 0:
        group = group // 2
        height = height + 1
    return height


def parent_of(group, slot, top):
    if slot == 0:
        return (group | 1, 1)
    height = front_height(group, top)
    if height == top + 1:
        return None
    if height == top:
        return (0, 1)
    reach = 2 ** (height - 1)
    if (group >> height) & 1 == 0:
        return (group + reach, 1)
    return (group - reach, 1)


def reference(factor_inverse, contribution, block_map, sep_size, right_side):
    top = N_SUB.bit_length() - 1
    fronts = [(group, 0) for group in range(N_SUB)] + [(group, 1) for group in range(N_SUB)]
    heights = {}
    children = {}
    for front in fronts:
        heights[front] = 0 if front[1] == 0 else front_height(front[0], top)
        children[front] = []
    for front in fronts:
        parent = parent_of(front[0], front[1], top)
        if parent is not None:
            children[parent].append(front)
    positions = jnp.arange(SEP, dtype=jnp.int32)

    def keeper(front):
        return (positions < sep_size[front[0], front[1]])[:, None].astype(jnp.float32)

    forward = {}
    for height in range(top + 2):
        for front in fronts:
            if heights[front] != height:
                continue
            residual = right_side[front[0], front[1]]
            for child in children[front]:
                product = jnp.dot(contribution[child[0], child[1]], forward[child].astype(jnp.bfloat16), preferred_element_type=jnp.float32)
                placed = jnp.zeros((BLOCKS, BLK, NRHS), jnp.float32).at[block_map[child[0], child[1]]].add(product.reshape(BLOCKS, BLK, NRHS))
                residual = residual - placed.reshape(SEP, NRHS)
            keep = keeper(front)
            residual = keep * residual
            forward[front] = keep * jnp.dot(factor_inverse[front[0], front[1]], residual.astype(jnp.bfloat16), preferred_element_type=jnp.float32)
    backward = {}
    for height in range(top + 1, -1, -1):
        for front in fronts:
            if heights[front] != height:
                continue
            keep = keeper(front)
            parent = parent_of(front[0], front[1], top)
            if parent is None:
                adjusted = forward[front]
            else:
                shaped = backward[parent].astype(jnp.bfloat16).reshape(BLOCKS, BLK, NRHS)
                picked = shaped[block_map[front[0], front[1]]].reshape(SEP, NRHS)
                carried = jnp.dot(contribution[front[0], front[1]].T, picked, preferred_element_type=jnp.float32)
                adjusted = keep * (forward[front] - carried)
            backward[front] = keep * jnp.dot(factor_inverse[front[0], front[1]].T, adjusted.astype(jnp.bfloat16), preferred_element_type=jnp.float32)
    return jnp.stack([jnp.stack([backward[(group, 0)], backward[(group, 1)]]) for group in range(N_SUB)])
```

```python
import functools

import jax
import jax.numpy as jnp
from jax import lax
from jax.experimental import pallas as pl
from jax.experimental.pallas import tpu as pltpu
from jax.sharding import PartitionSpec as P

MESH = pl.DeviceIdType.MESH
F32 = jnp.float32
BF16 = jnp.bfloat16


def tree(groups):
    levels = groups.bit_length() - 1
    heights, parents = [], []
    for g in range(groups):
        height = levels + 1
        if g:
            height = 1
            while (g >> (height - 1)) & 1 == 0:
                height += 1
        heights.append(height)
        if height == levels + 1:
            parents.append(0)
        elif height == levels:
            parents.append(0)
        else:
            reach = 2 ** (height - 1)
            parents.append(g + reach if (g >> height) & 1 == 0 else g - reach)
    first, second, slots = [], [], []
    for g in range(groups):
        kids = [c for c in range(1, groups) if parents[c] == g]
        first.append(kids[0] if kids else 0)
        second.append(kids[1] if len(kids) > 1 else -1)
        slots.append(0 if g == 0 else [c for c in range(1, groups) if parents[c] == parents[g]].index(g))
    return heights, parents, first, second, slots


def pick(table, index):
    value = jnp.int32(table[0])
    for position in range(1, len(table)):
        value = jnp.where(index == position, jnp.int32(table[position]), value)
    return value


def remote(src, dst, send, recv, device):
    return pltpu.make_async_remote_copy(
        src_ref=src, dst_ref=dst, send_sem=send, recv_sem=recv, device_id=device, device_id_type=MESH
    )


def loop(low, high, body):
    def step(index, carry):
        body(index)
        return carry

    lax.fori_loop(low, high, step, 0)


def kernel(
    groups, hi, lo,
    sep, inv, rhs, li_hbm, co_hbm, out,
    li, co0, co1, ag, agb, st, stb, p1, p1b, p2, p2b, cross, xb, ab, zs, acc, xs, acct,
    wsem, s_ag1, s_ag2, r_ag, s_1, r_1, s_2, r_2, s_x, r_x,
    s_b1, r_b1, s_b2, r_b2, s_par, s_gb1, s_gb2, r_gb, s_xb,
):
    heights, parents, first, second, slots = tree(groups)
    m = lax.axis_index("sub")
    f = lax.axis_index("front")
    h, l = f // lo, f % lo
    rows, n = rhs.shape[1], rhs.shape[2]
    co = (co0, co1)
    per = co0.shape[0] // (hi * lo)
    parent, slot = pick(parents, m), pick(slots, m)
    kid0, kid1 = pick(first, m), pick(second, m)
    top = m == 0
    odd = m % 2 == 1
    two = kid1 >= 0
    mate = jnp.where(odd, m - 1, m + 1)

    weights = [
        pltpu.make_async_copy(li_hbm.at[0], li.at[0], wsem.at[0]),
        pltpu.make_async_copy(co_hbm.at[0], co0, wsem.at[1]),
        pltpu.make_async_copy(li_hbm.at[1], li.at[1], wsem.at[2]),
        pltpu.make_async_copy(co_hbm.at[1], co1, wsem.at[3]),
    ]
    for weight in weights:
        weight.start()

    barrier = pltpu.get_barrier_semaphore()
    count = 0
    for d in range(1, hi):
        pl.semaphore_signal(barrier, inc=1, device_id=(m, (h + d) % hi * lo + l), device_id_type=MESH)
        count += 1
    for e in range(1, lo):
        pl.semaphore_signal(barrier, inc=1, device_id=(m, h * lo + (l + e) % lo), device_id_type=MESH)
        count += 1
    for g in range(1, groups):
        for d in range(hi):
            pl.semaphore_signal(
                barrier, inc=1, device_id=((m + g) % groups, (h + d) % hi * lo + l), device_id_type=MESH
            )
            count += 1

    def keep_rows(k):
        return f * rows + lax.broadcasted_iota(jnp.int32, (rows, n), 0) < sep[0, k]

    def keep_columns(k):
        return f * rows + lax.broadcasted_iota(jnp.int32, (n, rows), 1) < sep[0, k]

    def away(d):
        return (h + hi - d) % hi

    def peer(e):
        return h * lo + (l + e) % lo

    def blocks(k, q):
        return jnp.concatenate([co[k][inv[k, q * per + j]] for j in range(per)], axis=0)

    def columns(k, q):
        return li[k, :, pl.ds(pl.multiple_of(q * rows, rows), rows)]

    def ag_hi(k, d):
        return remote(ag.at[k, f], ag.at[k, f], s_ag1.at[k, d], r_ag.at[k, f], (m, (h + d) % hi * lo + l))

    def ag_lo(k, q, e, d):
        return remote(ag.at[k, q], ag.at[k, q], s_ag2.at[k, e, d], r_ag.at[k, q], (m, peer(e)))

    def gather(k, consume):
        for d in range(1, hi):
            ag_hi(k, d).start()
        for e in range(1, lo):
            ag_lo(k, f, e, 0).start()
        consume(f)

        def from_hi(d):
            q = away(d) * lo + l
            ag_lo(k, q, 0, 0).wait_recv()
            for e in range(1, lo):
                ag_lo(k, q, e, d).start()
            consume(q)

        loop(1, hi, from_hi)
        for e in range(1, lo):
            def from_lo(d):
                q = away(d) * lo + (l + lo - e) % lo
                ag_lo(k, q, 0, 0).wait_recv()
                consume(q)

            loop(0, hi, from_lo)

    def gather_sent(k):
        for d in range(1, hi):
            ag_hi(k, d).wait_send()
        for e in range(1, lo):
            loop(0, hi, lambda d: ag_lo(k, away(d) * lo + l, e, d).wait_send())

    def rs1(st_, p_, s_, r_, k, e, h2):
        q = h2 * lo + (l + e) % lo
        return remote(st_.at[k, q], p_.at[k, e, h2], s_.at[k, e, h2], r_.at[k, e, h2], (m, peer(e)))

    def reduce_lo(bufs, k, produce, finish, steps):
        st_, p_, s_, r_ = bufs
        for e in range(1, lo):
            def send(d):
                h2 = (h + 1 + d) % hi
                q = h2 * lo + (l + e) % lo
                st_[k, q] = produce(q).astype(BF16)
                rs1(st_, p_, s_, r_, k, e, h2).start()

            loop(0, hi, send)

        def total(h2):
            value = produce(h2 * lo + l)
            for e in range(1, lo):
                rs1(st_, p_, s_, r_, k, e, h2).wait_recv()
                value = value + p_[k, e, h2].astype(F32)
            return value.astype(BF16)

        def body(d):
            h2 = (h + 1 + d) % hi
            st_[k, h2 * lo + l] = total(h2)
            finish(h2)

        loop(0, steps, body)
        return total

    def reduce_sent(bufs, k):
        st_, p_, s_, r_ = bufs
        for e in range(1, lo):
            loop(0, hi, lambda h2: rs1(st_, p_, s_, r_, k, e, h2).wait_send())

    up = (st, p1, s_1, r_1)
    down = (stb, p1b, s_b1, r_b1)

    def rs2(k, c, dst, h2):
        return remote(st.at[k, h2 * lo + l], p2.at[c, h], s_2.at[k, h2], r_2.at[c, h], (dst, h2 * lo + l))

    def wait2(c, h2):
        remote(p2.at[c, h2], p2.at[c, h2], s_2.at[0, 0], r_2.at[c, h2], (mate, f)).wait_recv()

    def rs2b(k, h2):
        return remote(stb.at[k, h2 * lo + l], p2b.at[k, h], s_b2.at[k, h2], r_b2.at[k, h], (m, h2 * lo + l))

    def to_mate(q):
        return remote(st.at[0, q], cross.at[q], s_x.at[q], r_x.at[q], (mate, f))

    def solve(k):
        acc[...] = jnp.zeros_like(acc)

        def consume(q):
            acc[...] += jnp.dot(columns(k, q), ag[k, q], preferred_element_type=F32)

        return consume

    ag[0, f] = jnp.where(keep_rows(0), rhs[0], 0.0).astype(BF16)
    pl.semaphore_wait(barrier, count)
    weights[0].wait()
    gather(0, solve(0))
    leaf = jnp.where(keep_rows(0), acc[...], 0.0)
    xs[0] = leaf.T
    xb[...] = leaf.astype(BF16)
    weights[1].wait()

    def lifted(k):
        return lambda q: jnp.dot(blocks(k, q), xb[...], preferred_element_type=F32)

    @pl.when(jnp.logical_not(odd))
    def _():
        for e in list(range(1, lo)) + [0]:
            def send(d):
                q = (h + 1 + d) % hi * lo + (l + e) % lo
                st[0, q] = lifted(0)(q).astype(BF16)
                to_mate(q).start()

            loop(0, hi, send)

    @pl.when(odd)
    def _():
        def produce(q):
            value = lifted(0)(q)
            to_mate(q).wait_recv()
            return value + cross[q].astype(F32)

        total = reduce_lo(up, 0, produce, lambda h2: rs2(0, 0, m, h2).start(), hi - 1)
        p2[0, h] = total(h)
        loop(1, hi, lambda d: wait2(0, away(d)))

    @pl.when(jnp.logical_not(odd))
    def _():
        loop(0, hi, lambda h2: wait2(0, h2))

    incoming = p2[0, 0].astype(F32)
    for h2 in range(1, hi):
        incoming = incoming + p2[0, h2].astype(F32)
    acc[...] = rhs[1] - incoming

    @pl.when(two)
    def _():
        loop(0, hi, lambda h2: wait2(1, h2))
        other = p2[1, 0].astype(F32)
        for h2 in range(1, hi):
            other = other + p2[1, h2].astype(F32)
        acc[...] -= other

    ag[1, f] = jnp.where(keep_rows(1), acc[...], 0.0).astype(BF16)
    weights[2].wait()
    gather(1, solve(1))
    upper = jnp.where(keep_rows(1), acc[...], 0.0)
    xs[1] = upper.T
    xb[...] = upper.astype(BF16)
    weights[3].wait()

    def to_child(c, kid, h2):
        return remote(zs, agb.at[1, f], s_par.at[c, h2], r_gb.at[1, f], (kid, h2 * lo + l))

    def gb_lo(k, q, e, d):
        return remote(agb.at[k, q], agb.at[k, q], s_gb2.at[k, e, d], r_gb.at[k, q], (m, peer(e)))

    def gb_hi(d):
        return remote(agb.at[0, f], agb.at[0, f], s_gb1.at[d], r_gb.at[0, f], (m, (h + d) % hi * lo + l))

    def gb_mate(q):
        return remote(agb.at[0, q], agb.at[0, q], s_xb.at[q], r_gb.at[0, q], (mate, f))

    def carry(k, q):
        acct[...] += jnp.dot(agb[k, q], blocks(k, q), preferred_element_type=F32)

    acct[...] = jnp.zeros_like(acct)

    @pl.when(jnp.logical_not(top))
    def _():
        reduce_lo(up, 1, lifted(1), lambda h2: rs2(1, slot, parent, h2).start(), hi)

        def from_parent(d):
            q = away(d) * lo + l
            gb_lo(1, q, 0, 0).wait_recv()
            for e in range(1, lo):
                gb_lo(1, q, e, d).start()
            carry(1, q)

        loop(0, hi, from_parent)
        for e in range(1, lo):
            def from_lo(d):
                q = away(d) * lo + (l + lo - e) % lo
                gb_lo(1, q, 0, 0).wait_recv()
                carry(1, q)

            loop(0, hi, from_lo)

    def descend(k):
        ab[...] = jnp.where(keep_columns(k), xs[k] - acct[...], 0.0).astype(BF16)

        def produce(q):
            return jnp.dot(ab[...], columns(k, q), preferred_element_type=F32)

        total = reduce_lo(down, k, produce, lambda h2: rs2b(k, h2).start(), hi - 1)
        value = total(h).astype(F32)

        def collect(d):
            source = away(d)
            remote(
                p2b.at[k, source], p2b.at[k, source], s_b2.at[k, 0], r_b2.at[k, source], (mate, f)
            ).wait_recv()
            return p2b[k, source].astype(F32)

        for d in range(1, hi):
            value = value + collect(d)
        return jnp.where(keep_columns(k), value, 0.0)

    solved = descend(1)
    zs[...] = solved.astype(BF16)

    @pl.when(jnp.logical_not(odd))
    def _():
        loop(0, hi, lambda d: to_child(0, kid0, (h + d) % hi).start())

    @pl.when(two)
    def _():
        loop(0, hi, lambda d: to_child(1, kid1, (h + d) % hi).start())

    acct[...] = jnp.zeros_like(acct)

    @pl.when(odd)
    def _():
        agb[0, f] = zs[...]
        for d in range(1, hi):
            gb_hi(d).start()
        for e in range(1, lo):
            gb_lo(0, f, e, 0).start()
        gb_mate(f).start()
        carry(0, f)

        def from_hi(d):
            q = away(d) * lo + l
            gb_lo(0, q, 0, 0).wait_recv()
            for e in range(1, lo):
                gb_lo(0, q, e, d).start()
            gb_mate(q).start()
            carry(0, q)

        loop(1, hi, from_hi)
        for e in range(1, lo):
            def from_lo(d):
                q = away(d) * lo + (l + lo - e) % lo
                gb_lo(0, q, 0, 0).wait_recv()
                gb_mate(q).start()
                carry(0, q)

            loop(0, hi, from_lo)

    out[1] = solved.T

    @pl.when(jnp.logical_not(odd))
    def _():
        for e in range(lo):
            def from_mate(d):
                q = away(d) * lo + (l + lo - e) % lo
                gb_lo(0, q, 0, 0).wait_recv()
                carry(0, q)

            loop(0, hi, from_mate)

    out[0] = descend(0).T

    for k in range(2):
        gather_sent(k)
        reduce_sent(down, k)
        loop(1, hi, lambda d: rs2b(k, (h + d) % hi).wait_send())

    @pl.when(jnp.logical_not(top))
    def _():
        reduce_sent(up, 1)
        loop(0, hi, lambda h2: rs2(1, slot, parent, h2).wait_send())
        for e in range(1, lo):
            loop(0, hi, lambda d: gb_lo(1, away(d) * lo + l, e, d).wait_send())

    @pl.when(jnp.logical_not(odd))
    def _():
        loop(0, hi * lo, lambda q: to_mate(q).wait_send())
        loop(0, hi, lambda d: to_child(0, kid0, (h + d) % hi).wait_send())

    @pl.when(two)
    def _():
        loop(0, hi, lambda d: to_child(1, kid1, (h + d) % hi).wait_send())

    @pl.when(odd)
    def _():
        reduce_sent(up, 0)
        loop(1, hi, lambda d: rs2(0, 0, m, (h + d) % hi).wait_send())
        for d in range(1, hi):
            gb_hi(d).wait_send()
        for e in range(1, lo):
            loop(0, hi, lambda d: gb_lo(0, away(d) * lo + l, e, d).wait_send())
        loop(0, hi * lo, lambda q: gb_mate(q).wait_send())


def per_device(hi, lo, factor_inverse, contribution, block_map, sep_size, right_side):
    groups = lax.axis_size("sub")
    rows, n = right_side.shape[2:]
    sep_rows = contribution.shape[2]
    count = block_map.shape[2]
    fronts = hi * lo
    steps = jnp.arange(count, dtype=jnp.int32)
    inverse = jnp.sum(
        jnp.where(block_map[0][:, :, None] == steps[None, None, :], steps[None, :, None], 0), axis=1
    )
    dma = pltpu.SemaphoreType.DMA
    vmem = pl.BlockSpec(memory_space=pltpu.VMEM)
    smem = pl.BlockSpec(memory_space=pltpu.SMEM)
    hbm = pl.BlockSpec(memory_space=pl.ANY)
    out = pl.pallas_call(
        functools.partial(kernel, groups, hi, lo),
        out_shape=jax.ShapeDtypeStruct((2, rows, n), F32),
        in_specs=[smem, smem, vmem, hbm, hbm],
        out_specs=vmem,
        scratch_shapes=[
            pltpu.VMEM((2, rows, sep_rows), BF16),
            pltpu.VMEM((count, sep_rows // count, rows), BF16),
            pltpu.VMEM((count, sep_rows // count, rows), BF16),
            pltpu.VMEM((2, fronts, rows, n), BF16),
            pltpu.VMEM((2, fronts, n, rows), BF16),
            pltpu.VMEM((2, fronts, rows, n), BF16),
            pltpu.VMEM((2, fronts, n, rows), BF16),
            pltpu.VMEM((2, lo, hi, rows, n), BF16),
            pltpu.VMEM((2, lo, hi, n, rows), BF16),
            pltpu.VMEM((2, hi, rows, n), BF16),
            pltpu.VMEM((2, hi, n, rows), BF16),
            pltpu.VMEM((fronts, rows, n), BF16),
            pltpu.VMEM((rows, n), BF16),
            pltpu.VMEM((n, rows), BF16),
            pltpu.VMEM((n, rows), BF16),
            pltpu.VMEM((rows, n), F32),
            pltpu.VMEM((2, n, rows), F32),
            pltpu.VMEM((n, rows), F32),
            dma((4,)),
            dma((2, hi)), dma((2, lo, hi)), dma((2, fronts)),
            dma((2, lo, hi)), dma((2, lo, hi)),
            dma((2, hi)), dma((2, hi)),
            dma((fronts,)), dma((fronts,)),
            dma((2, lo, hi)), dma((2, lo, hi)),
            dma((2, hi)), dma((2, hi)),
            dma((2, hi)), dma((hi,)), dma((2, lo, hi)), dma((2, fronts)), dma((fronts,)),
        ],
        compiler_params=pltpu.CompilerParams(
            collective_id=0, has_side_effects=True, vmem_limit_bytes=56 * 1024 * 1024
        ),
    )(
        sep_size,
        inverse,
        right_side[0],
        factor_inverse[0],
        contribution[0].reshape(2, count, sep_rows // count, rows),
    )
    return out[None]


def solution(mesh):
    fronts = mesh.shape["front"]
    hi = min(4, fronts)
    placed = (
        P("sub", None, "front", None),
        P("sub", None, None, "front"),
        P("sub", None, None),
        P("sub", None),
        P("sub", None, "front", None),
    )
    return jax.shard_map(
        functools.partial(per_device, hi, fronts // hi),
        mesh=mesh,
        in_specs=placed,
        out_specs=P("sub", None, "front", None),
        check_vma=False,
    )
```

```python
import functools

import jax
import jax.numpy as jnp
from jax import lax
from jax.experimental import pallas as pl
from jax.experimental.pallas import tpu as pltpu
from jax.sharding import PartitionSpec as P

MESH = pl.DeviceIdType.MESH
F32 = jnp.float32
BF16 = jnp.bfloat16


def tree(groups):
    levels = groups.bit_length() - 1
    heights, parents = [], []
    for g in range(groups):
        height = levels + 1
        if g:
            height = 1
            while (g >> (height - 1)) & 1 == 0:
                height += 1
        heights.append(height)
        if height == levels + 1:
            parents.append(0)
        elif height == levels:
            parents.append(0)
        else:
            reach = 2 ** (height - 1)
            parents.append(g + reach if (g >> height) & 1 == 0 else g - reach)
    first, second, slots = [], [], []
    for g in range(groups):
        kids = [c for c in range(1, groups) if parents[c] == g]
        first.append(kids[0] if kids else 0)
        second.append(kids[1] if len(kids) > 1 else -1)
        slots.append(0 if g == 0 else [c for c in range(1, groups) if parents[c] == parents[g]].index(g))
    return heights, parents, first, second, slots


def pick(table, index):
    value = table[0] + jnp.int32(0)
    for position in range(1, len(table)):
        value = jnp.where(index == position, table[position] + jnp.int32(0), value)
    return value


def remote(src, dst, send, recv, device):
    return pltpu.make_async_remote_copy(
        src_ref=src, dst_ref=dst, send_sem=send, recv_sem=recv, device_id=device, device_id_type=MESH
    )


def loop(low, high, body):
    def step(index, carry):
        body(index)
        return carry

    lax.fori_loop(low, high, step, 0)


def kernel(
    groups, hi, lo,
    sep, inv, rhs, li_hbm, co_hbm, out,
    li, co0, co1, ag, agb, st, stb, p1, p1b, p2, p2b, cross, xb, ab, zs, acc, xs, acct,
    wsem, s_ag1, s_ag2, r_ag, s_1, r_1, s_2, r_2, s_x, r_x,
    s_b1, r_b1, s_b2, r_b2, s_par, s_gb1, s_gb2, r_gb, s_xb,
):
    heights, parents, first, second, slots = tree(groups)
    m = lax.axis_index("sub")
    f = lax.axis_index("front")
    h, l = f // lo, f % lo
    rows, n = rhs.shape[1], rhs.shape[2]
    co = (co0, co1)
    per = co0.shape[0] // (hi * lo)
    parent, slot = pick(parents, m), pick(slots, m)
    kid0, kid1 = pick(first, m), pick(second, m)
    top = m == 0
    odd = m % 2 == 1
    two = kid1 >= 0
    mate = jnp.where(odd, m - 1, m + 1)

    weights = [
        pltpu.make_async_copy(li_hbm.at[0], li.at[0], wsem.at[0]),
        pltpu.make_async_copy(co_hbm.at[0], co0, wsem.at[1]),
        pltpu.make_async_copy(li_hbm.at[1], li.at[1], wsem.at[2]),
        pltpu.make_async_copy(co_hbm.at[1], co1, wsem.at[3]),
    ]
    for weight in weights:
        weight.start()

    barrier = pltpu.get_barrier_semaphore()
    count = 0
    for d in range(1, hi):
        pl.semaphore_signal(barrier, inc=1, device_id=(m, (h + d) % hi * lo + l), device_id_type=MESH)
        count += 1
    for e in range(1, lo):
        pl.semaphore_signal(barrier, inc=1, device_id=(m, h * lo + (l + e) % lo), device_id_type=MESH)
        count += 1
    for g in range(1, groups):
        for d in range(hi):
            pl.semaphore_signal(
                barrier, inc=1, device_id=((m + g) % groups, (h + d) % hi * lo + l), device_id_type=MESH
            )
            count += 1

    def keep_rows(k):
        return f * rows + lax.broadcasted_iota(jnp.int32, (rows, n), 0) < sep[0, k]

    def keep_columns(k):
        return f * rows + lax.broadcasted_iota(jnp.int32, (n, rows), 1) < sep[0, k]

    order = [sorted(range(hi), key=lambda other: (abs(other - own), other)) for own in range(hi)]
    nearest = [pick([order[own][d] for own in range(hi)], h) for d in range(hi)]

    def near(d):
        if isinstance(d, int):
            return nearest[d]
        return pick(nearest, d)

    def peer(e):
        return h * lo + (l + e) % lo

    def blocks(k, q):
        return jnp.concatenate([co[k][inv[k, q * per + j]] for j in range(per)], axis=0)

    def columns(k, q):
        return li[k, :, pl.ds(pl.multiple_of(q * rows, rows), rows)]

    def ag_hi(k, d):
        return remote(ag.at[k, f], ag.at[k, f], s_ag1.at[k, d], r_ag.at[k, f], (m, near(d) * lo + l))

    def ag_lo(k, q, e, d):
        return remote(ag.at[k, q], ag.at[k, q], s_ag2.at[k, e, d], r_ag.at[k, q], (m, peer(e)))

    def gather(k, consume):
        for d in range(1, hi):
            ag_hi(k, d).start()
        for e in range(1, lo):
            ag_lo(k, f, e, 0).start()
        consume(f)

        def from_hi(d):
            q = near(d) * lo + l
            ag_lo(k, q, 0, 0).wait_recv()
            for e in range(1, lo):
                ag_lo(k, q, e, d).start()
            consume(q)

        loop(1, hi, from_hi)
        for e in range(1, lo):
            def from_lo(d):
                q = near(d) * lo + (l + lo - e) % lo
                ag_lo(k, q, 0, 0).wait_recv()
                consume(q)

            loop(0, hi, from_lo)

    def gather_sent(k):
        for d in range(1, hi):
            ag_hi(k, d).wait_send()
        for e in range(1, lo):
            loop(0, hi, lambda d: ag_lo(k, near(d) * lo + l, e, d).wait_send())

    def rs1(st_, p_, s_, r_, k, e, h2):
        q = h2 * lo + (l + e) % lo
        return remote(st_.at[k, q], p_.at[k, e, h2], s_.at[k, e, h2], r_.at[k, e, h2], (m, peer(e)))

    def reduce_lo(bufs, k, produce, finish, steps):
        st_, p_, s_, r_ = bufs
        for e in range(1, lo):
            def send(d):
                h2 = near((d + 1) % hi)
                q = h2 * lo + (l + e) % lo
                st_[k, q] = produce(q).astype(BF16)
                rs1(st_, p_, s_, r_, k, e, h2).start()

            loop(0, hi, send)

        def total(h2):
            value = produce(h2 * lo + l)
            for e in range(1, lo):
                rs1(st_, p_, s_, r_, k, e, h2).wait_recv()
                value = value + p_[k, e, h2].astype(F32)
            return value.astype(BF16)

        def body(d):
            h2 = near((d + 1) % hi)
            st_[k, h2 * lo + l] = total(h2)
            finish(h2)

        loop(0, steps, body)
        return total

    def reduce_sent(bufs, k):
        st_, p_, s_, r_ = bufs
        for e in range(1, lo):
            loop(0, hi, lambda h2: rs1(st_, p_, s_, r_, k, e, h2).wait_send())

    up = (st, p1, s_1, r_1)
    down = (stb, p1b, s_b1, r_b1)

    def rs2(k, c, dst, h2):
        return remote(st.at[k, h2 * lo + l], p2.at[c, h], s_2.at[k, h2], r_2.at[c, h], (dst, h2 * lo + l))

    def wait2(c, h2):
        remote(p2.at[c, h2], p2.at[c, h2], s_2.at[0, 0], r_2.at[c, h2], (mate, f)).wait_recv()

    def rs2b(k, h2):
        return remote(stb.at[k, h2 * lo + l], p2b.at[k, h], s_b2.at[k, h2], r_b2.at[k, h], (m, h2 * lo + l))

    def to_mate(q):
        return remote(st.at[0, q], cross.at[q], s_x.at[q], r_x.at[q], (mate, f))

    def solve(k):
        acc[...] = jnp.zeros_like(acc)

        def consume(q):
            acc[...] += jnp.dot(columns(k, q), ag[k, q], preferred_element_type=F32)

        return consume

    ag[0, f] = jnp.where(keep_rows(0), rhs[0], 0.0).astype(BF16)
    pl.semaphore_wait(barrier, count)
    weights[0].wait()
    gather(0, solve(0))
    leaf = jnp.where(keep_rows(0), acc[...], 0.0)
    xs[0] = leaf.T
    xb[...] = leaf.astype(BF16)
    weights[1].wait()

    def lifted(k):
        return lambda q: jnp.dot(blocks(k, q), xb[...], preferred_element_type=F32)

    @pl.when(jnp.logical_not(odd))
    def _():
        for e in list(range(1, lo)) + [0]:
            def send(d):
                q = near((d + 1) % hi) * lo + (l + e) % lo
                st[0, q] = lifted(0)(q).astype(BF16)
                to_mate(q).start()

            loop(0, hi, send)

    @pl.when(odd)
    def _():
        def produce(q):
            value = lifted(0)(q)
            to_mate(q).wait_recv()
            return value + cross[q].astype(F32)

        total = reduce_lo(up, 0, produce, lambda h2: rs2(0, 0, m, h2).start(), hi - 1)
        p2[0, h] = total(h)
        loop(1, hi, lambda d: wait2(0, near(d)))

    @pl.when(jnp.logical_not(odd))
    def _():
        loop(0, hi, lambda h2: wait2(0, h2))

    incoming = p2[0, 0].astype(F32)
    for h2 in range(1, hi):
        incoming = incoming + p2[0, h2].astype(F32)
    acc[...] = rhs[1] - incoming

    @pl.when(two)
    def _():
        loop(0, hi, lambda h2: wait2(1, h2))
        other = p2[1, 0].astype(F32)
        for h2 in range(1, hi):
            other = other + p2[1, h2].astype(F32)
        acc[...] -= other

    ag[1, f] = jnp.where(keep_rows(1), acc[...], 0.0).astype(BF16)
    weights[2].wait()
    gather(1, solve(1))
    upper = jnp.where(keep_rows(1), acc[...], 0.0)
    xs[1] = upper.T
    xb[...] = upper.astype(BF16)
    weights[3].wait()

    def to_child(c, kid, h2):
        return remote(zs, agb.at[1, f], s_par.at[c, h2], r_gb.at[1, f], (kid, h2 * lo + l))

    def gb_lo(k, q, e, d):
        return remote(agb.at[k, q], agb.at[k, q], s_gb2.at[k, e, d], r_gb.at[k, q], (m, peer(e)))

    def gb_hi(d):
        return remote(agb.at[0, f], agb.at[0, f], s_gb1.at[d], r_gb.at[0, f], (m, near(d) * lo + l))

    def gb_mate(q):
        return remote(agb.at[0, q], agb.at[0, q], s_xb.at[q], r_gb.at[0, q], (mate, f))

    def carry(k, q):
        acct[...] += jnp.dot(agb[k, q], blocks(k, q), preferred_element_type=F32)

    acct[...] = jnp.zeros_like(acct)

    @pl.when(jnp.logical_not(top))
    def _():
        reduce_lo(up, 1, lifted(1), lambda h2: rs2(1, slot, parent, h2).start(), hi)

        def from_parent(d):
            q = near(d) * lo + l
            gb_lo(1, q, 0, 0).wait_recv()
            for e in range(1, lo):
                gb_lo(1, q, e, d).start()
            carry(1, q)

        loop(0, hi, from_parent)
        for e in range(1, lo):
            def from_lo(d):
                q = near(d) * lo + (l + lo - e) % lo
                gb_lo(1, q, 0, 0).wait_recv()
                carry(1, q)

            loop(0, hi, from_lo)

    def descend(k):
        ab[...] = jnp.where(keep_columns(k), xs[k] - acct[...], 0.0).astype(BF16)

        def produce(q):
            return jnp.dot(ab[...], columns(k, q), preferred_element_type=F32)

        total = reduce_lo(down, k, produce, lambda h2: rs2b(k, h2).start(), hi - 1)
        value = total(h).astype(F32)

        def collect(d):
            source = near(d)
            remote(
                p2b.at[k, source], p2b.at[k, source], s_b2.at[k, 0], r_b2.at[k, source], (mate, f)
            ).wait_recv()
            return p2b[k, source].astype(F32)

        for d in range(1, hi):
            value = value + collect(d)
        return jnp.where(keep_columns(k), value, 0.0)

    solved = descend(1)
    zs[...] = solved.astype(BF16)

    @pl.when(jnp.logical_not(odd))
    def _():
        loop(0, hi, lambda d: to_child(0, kid0, near(d)).start())

    @pl.when(two)
    def _():
        loop(0, hi, lambda d: to_child(1, kid1, near(d)).start())

    acct[...] = jnp.zeros_like(acct)

    @pl.when(odd)
    def _():
        agb[0, f] = zs[...]
        for d in range(1, hi):
            gb_hi(d).start()
        for e in range(1, lo):
            gb_lo(0, f, e, 0).start()
        gb_mate(f).start()
        carry(0, f)

        def from_hi(d):
            q = near(d) * lo + l
            gb_lo(0, q, 0, 0).wait_recv()
            for e in range(1, lo):
                gb_lo(0, q, e, d).start()
            gb_mate(q).start()
            carry(0, q)

        loop(1, hi, from_hi)
        for e in range(1, lo):
            def from_lo(d):
                q = near(d) * lo + (l + lo - e) % lo
                gb_lo(0, q, 0, 0).wait_recv()
                gb_mate(q).start()
                carry(0, q)

            loop(0, hi, from_lo)

    out[1] = solved.T

    @pl.when(jnp.logical_not(odd))
    def _():
        for e in range(lo):
            def from_mate(d):
                q = near(d) * lo + (l + lo - e) % lo
                gb_lo(0, q, 0, 0).wait_recv()
                carry(0, q)

            loop(0, hi, from_mate)

    out[0] = descend(0).T

    for k in range(2):
        gather_sent(k)
        reduce_sent(down, k)
        loop(1, hi, lambda d: rs2b(k, (h + d) % hi).wait_send())

    @pl.when(jnp.logical_not(top))
    def _():
        reduce_sent(up, 1)
        loop(0, hi, lambda h2: rs2(1, slot, parent, h2).wait_send())
        for e in range(1, lo):
            loop(0, hi, lambda d: gb_lo(1, near(d) * lo + l, e, d).wait_send())

    @pl.when(jnp.logical_not(odd))
    def _():
        loop(0, hi * lo, lambda q: to_mate(q).wait_send())
        loop(0, hi, lambda d: to_child(0, kid0, near(d)).wait_send())

    @pl.when(two)
    def _():
        loop(0, hi, lambda d: to_child(1, kid1, near(d)).wait_send())

    @pl.when(odd)
    def _():
        reduce_sent(up, 0)
        loop(1, hi, lambda d: rs2(0, 0, m, (h + d) % hi).wait_send())
        for d in range(1, hi):
            gb_hi(d).wait_send()
        for e in range(1, lo):
            loop(0, hi, lambda d: gb_lo(0, near(d) * lo + l, e, d).wait_send())
        loop(0, hi * lo, lambda q: gb_mate(q).wait_send())


def per_device(hi, lo, factor_inverse, contribution, block_map, sep_size, right_side):
    groups = lax.axis_size("sub")
    rows, n = right_side.shape[2:]
    sep_rows = contribution.shape[2]
    count = block_map.shape[2]
    fronts = hi * lo
    steps = jnp.arange(count, dtype=jnp.int32)
    inverse = jnp.sum(
        jnp.where(block_map[0][:, :, None] == steps[None, None, :], steps[None, :, None], 0), axis=1
    )
    dma = pltpu.SemaphoreType.DMA
    vmem = pl.BlockSpec(memory_space=pltpu.VMEM)
    smem = pl.BlockSpec(memory_space=pltpu.SMEM)
    hbm = pl.BlockSpec(memory_space=pl.ANY)
    out = pl.pallas_call(
        functools.partial(kernel, groups, hi, lo),
        out_shape=jax.ShapeDtypeStruct((2, rows, n), F32),
        in_specs=[smem, smem, vmem, hbm, hbm],
        out_specs=vmem,
        scratch_shapes=[
            pltpu.VMEM((2, rows, sep_rows), BF16),
            pltpu.VMEM((count, sep_rows // count, rows), BF16),
            pltpu.VMEM((count, sep_rows // count, rows), BF16),
            pltpu.VMEM((2, fronts, rows, n), BF16),
            pltpu.VMEM((2, fronts, n, rows), BF16),
            pltpu.VMEM((2, fronts, rows, n), BF16),
            pltpu.VMEM((2, fronts, n, rows), BF16),
            pltpu.VMEM((2, lo, hi, rows, n), BF16),
            pltpu.VMEM((2, lo, hi, n, rows), BF16),
            pltpu.VMEM((2, hi, rows, n), BF16),
            pltpu.VMEM((2, hi, n, rows), BF16),
            pltpu.VMEM((fronts, rows, n), BF16),
            pltpu.VMEM((rows, n), BF16),
            pltpu.VMEM((n, rows), BF16),
            pltpu.VMEM((n, rows), BF16),
            pltpu.VMEM((rows, n), F32),
            pltpu.VMEM((2, n, rows), F32),
            pltpu.VMEM((n, rows), F32),
            dma((4,)),
            dma((2, hi)), dma((2, lo, hi)), dma((2, fronts)),
            dma((2, lo, hi)), dma((2, lo, hi)),
            dma((2, hi)), dma((2, hi)),
            dma((fronts,)), dma((fronts,)),
            dma((2, lo, hi)), dma((2, lo, hi)),
            dma((2, hi)), dma((2, hi)),
            dma((2, hi)), dma((hi,)), dma((2, lo, hi)), dma((2, fronts)), dma((fronts,)),
        ],
        compiler_params=pltpu.CompilerParams(
            collective_id=0, has_side_effects=True, vmem_limit_bytes=56 * 1024 * 1024
        ),
    )(
        sep_size,
        inverse,
        right_side[0],
        factor_inverse[0],
        contribution[0].reshape(2, count, sep_rows // count, rows),
    )
    return out[None]


def solution(mesh):
    fronts = mesh.shape["front"]
    hi = min(4, fronts)
    placed = (
        P("sub", None, "front", None),
        P("sub", None, None, "front"),
        P("sub", None, None),
        P("sub", None),
        P("sub", None, "front", None),
    )
    return jax.shard_map(
        functools.partial(per_device, hi, fronts // hi),
        mesh=mesh,
        in_specs=placed,
        out_specs=P("sub", None, "front", None),
        check_vma=False,
    )
```

```python
import functools

import jax
import jax.numpy as jnp
from jax import lax
from jax.experimental import pallas as pl
from jax.experimental.pallas import tpu as pltpu
from jax.sharding import PartitionSpec as P

MESH = pl.DeviceIdType.MESH
F32 = jnp.float32
BF16 = jnp.bfloat16


def tree(groups):
    levels = groups.bit_length() - 1
    heights, parents = [], []
    for g in range(groups):
        height = levels + 1
        if g:
            height = 1
            while (g >> (height - 1)) & 1 == 0:
                height += 1
        heights.append(height)
        if height == levels + 1:
            parents.append(0)
        elif height == levels:
            parents.append(0)
        else:
            reach = 2 ** (height - 1)
            parents.append(g + reach if (g >> height) & 1 == 0 else g - reach)
    first, second, slots = [], [], []
    for g in range(groups):
        kids = [c for c in range(1, groups) if parents[c] == g]
        first.append(kids[0] if kids else 0)
        second.append(kids[1] if len(kids) > 1 else -1)
        slots.append(0 if g == 0 else [c for c in range(1, groups) if parents[c] == parents[g]].index(g))
    return heights, parents, first, second, slots


def pick(table, index):
    value = table[0] + jnp.int32(0)
    for position in range(1, len(table)):
        value = jnp.where(index == position, table[position] + jnp.int32(0), value)
    return value


def remote(src, dst, send, recv, device):
    return pltpu.make_async_remote_copy(
        src_ref=src, dst_ref=dst, send_sem=send, recv_sem=recv, device_id=device, device_id_type=MESH
    )


def loop(low, high, body):
    def step(index, carry):
        body(index)
        return carry

    lax.fori_loop(low, high, step, 0)


def kernel(
    groups, hi, lo,
    sep, inv, rhs, li_hbm, co_hbm, out,
    li, co0, co1, ag, agb, st, stb, p1, p1b, p2, p2b, cross, xb, ab, zs, acc, xs, acct,
    wsem, s_ag1, s_ag2, r_ag, s_1, r_1, s_2, r_2, s_x, r_x,
    s_b1, r_b1, s_b2, r_b2, s_par, s_gb1, s_gb2, r_gb, s_xb,
):
    heights, parents, first, second, slots = tree(groups)
    m = lax.axis_index("sub")
    f = lax.axis_index("front")
    h, l = f // lo, f % lo
    rows, n = rhs.shape[1], rhs.shape[2]
    co = (co0, co1)
    per = co0.shape[0] // (hi * lo)
    parent, slot = pick(parents, m), pick(slots, m)
    kid0, kid1 = pick(first, m), pick(second, m)
    top = m == 0
    odd = m % 2 == 1
    two = kid1 >= 0
    mate = jnp.where(odd, m - 1, m + 1)

    weights = [
        pltpu.make_async_copy(li_hbm.at[0], li.at[0], wsem.at[0]),
        pltpu.make_async_copy(co_hbm.at[0], co0, wsem.at[1]),
        pltpu.make_async_copy(li_hbm.at[1], li.at[1], wsem.at[2]),
        pltpu.make_async_copy(co_hbm.at[1], co1, wsem.at[3]),
    ]
    for weight in weights:
        weight.start()

    barrier = pltpu.get_barrier_semaphore()
    count = 0
    for d in range(1, hi):
        pl.semaphore_signal(barrier, inc=1, device_id=(m, (h + d) % hi * lo + l), device_id_type=MESH)
        count += 1
    for e in range(1, lo):
        pl.semaphore_signal(barrier, inc=1, device_id=(m, h * lo + (l + e) % lo), device_id_type=MESH)
        count += 1
    for g in range(1, groups):
        for d in range(hi):
            pl.semaphore_signal(
                barrier, inc=1, device_id=((m + g) % groups, (h + d) % hi * lo + l), device_id_type=MESH
            )
            count += 1

    def keep_rows(k):
        return f * rows + lax.broadcasted_iota(jnp.int32, (rows, n), 0) < sep[0, k]

    def keep_columns(k):
        return f * rows + lax.broadcasted_iota(jnp.int32, (n, rows), 1) < sep[0, k]

    order = [sorted(range(hi), key=lambda other: (abs(other - own), other)) for own in range(hi)]
    nearest = [pick([order[own][d] for own in range(hi)], h) for d in range(hi)]

    def near(d):
        if isinstance(d, int):
            return nearest[d]
        return pick(nearest, d)

    def peer(e):
        return h * lo + (l + e) % lo

    def blocks(k, q):
        return jnp.concatenate([co[k][inv[k, q * per + j]] for j in range(per)], axis=0)

    def columns(k, q):
        return li[k, :, pl.ds(pl.multiple_of(q * rows, rows), rows)]

    def ag_hi(k, d):
        return remote(ag.at[k, f], ag.at[k, f], s_ag1.at[k, d], r_ag.at[k, f], (m, near(d) * lo + l))

    def ag_lo(k, q, e, d):
        return remote(ag.at[k, q], ag.at[k, q], s_ag2.at[k, e, d], r_ag.at[k, q], (m, peer(e)))

    def gather(k, consume, weight):
        for d in range(1, hi):
            pl.when(near(d) > h)(lambda: ag_hi(k, d).start())
        for e in range(1, lo):
            ag_lo(k, f, e, 0).start()
        weight.wait()
        consume(f)

        def from_hi(d):
            @pl.when(near(d) < h)
            def _():
                q = near(d) * lo + l
                ag_lo(k, q, 0, 0).wait_recv()
                for e in range(1, lo):
                    ag_lo(k, q, e, d).start()
                consume(q)

        loop(1, hi, from_hi)
        for e in range(1, lo):
            def from_lo(d):
                @pl.when(near(d) <= h)
                def _():
                    q = near(d) * lo + (l + lo - e) % lo
                    ag_lo(k, q, 0, 0).wait_recv()
                    consume(q)

            loop(0, hi, from_lo)

    def gather_sent(k):
        for d in range(1, hi):
            pl.when(near(d) > h)(lambda: ag_hi(k, d).wait_send())
        for e in range(1, lo):
            def forwarded(d):
                pl.when(near(d) <= h)(lambda: ag_lo(k, near(d) * lo + l, e, d).wait_send())

            loop(0, hi, forwarded)

    def rs1(st_, p_, s_, r_, k, e, h2):
        q = h2 * lo + (l + e) % lo
        return remote(st_.at[k, q], p_.at[k, e, h2], s_.at[k, e, h2], r_.at[k, e, h2], (m, peer(e)))

    def reduce_lo(bufs, k, produce, finish, steps, needed=lambda h2: h2 >= 0):
        st_, p_, s_, r_ = bufs
        for e in range(1, lo):
            def send(d):
                h2 = near((d + 1) % hi)
                q = h2 * lo + (l + e) % lo

                @pl.when(needed(h2))
                def _():
                    st_[k, q] = produce(q).astype(BF16)
                    rs1(st_, p_, s_, r_, k, e, h2).start()

            loop(0, hi, send)

        def total(h2):
            value = produce(h2 * lo + l)
            for e in range(1, lo):
                rs1(st_, p_, s_, r_, k, e, h2).wait_recv()
                value = value + p_[k, e, h2].astype(F32)
            return value.astype(BF16)

        def body(d):
            h2 = near((d + 1) % hi)

            @pl.when(needed(h2))
            def _():
                st_[k, h2 * lo + l] = total(h2)
                finish(h2)

        loop(0, steps, body)
        return total

    def reduce_sent(bufs, k, needed=lambda h2: h2 >= 0):
        st_, p_, s_, r_ = bufs
        for e in range(1, lo):
            def gone(h2):
                pl.when(needed(h2))(lambda: rs1(st_, p_, s_, r_, k, e, h2).wait_send())

            loop(0, hi, gone)

    up = (st, p1, s_1, r_1)
    down = (stb, p1b, s_b1, r_b1)

    def rs2(k, c, dst, h2):
        return remote(st.at[k, h2 * lo + l], p2.at[c, h], s_2.at[k, h2], r_2.at[c, h], (dst, h2 * lo + l))

    def wait2(c, h2):
        remote(p2.at[c, h2], p2.at[c, h2], s_2.at[0, 0], r_2.at[c, h2], (mate, f)).wait_recv()

    def rs2b(k, h2):
        return remote(stb.at[k, h2 * lo + l], p2b.at[k, h], s_b2.at[k, h2], r_b2.at[k, h], (m, h2 * lo + l))

    def to_mate(q):
        return remote(st.at[0, q], cross.at[q], s_x.at[q], r_x.at[q], (mate, f))

    def solve(k):
        acc[...] = jnp.zeros_like(acc)

        def consume(q):
            acc[...] += jnp.dot(columns(k, q), ag[k, q], preferred_element_type=F32)

        return consume

    ag[0, f] = jnp.where(keep_rows(0), rhs[0], 0.0).astype(BF16)
    pl.semaphore_wait(barrier, count)
    gather(0, solve(0), weights[0])
    leaf = jnp.where(keep_rows(0), acc[...], 0.0)
    xb[...] = leaf.astype(BF16)
    weights[1].wait()

    def hold(k):
        xs[k] = jnp.where(keep_rows(k), acc[...], 0.0).T

    def lifted(k):
        return lambda q: jnp.dot(blocks(k, q), xb[...], preferred_element_type=F32)

    @pl.when(jnp.logical_not(odd))
    def _():
        for e in list(range(1, lo)) + [0]:
            def send(d):
                q = near((d + 1) % hi) * lo + (l + e) % lo
                st[0, q] = lifted(0)(q).astype(BF16)
                to_mate(q).start()

            loop(0, hi, send)

    @pl.when(odd)
    def _():
        def produce(q):
            value = lifted(0)(q)
            to_mate(q).wait_recv()
            return value + cross[q].astype(F32)

        total = reduce_lo(up, 0, produce, lambda h2: rs2(0, 0, m, h2).start(), hi - 1)
        p2[0, h] = total(h)
        hold(0)
        loop(1, hi, lambda d: wait2(0, near(d)))

    @pl.when(jnp.logical_not(odd))
    def _():
        hold(0)
        loop(0, hi, lambda h2: wait2(0, h2))

    incoming = p2[0, 0].astype(F32)
    for h2 in range(1, hi):
        incoming = incoming + p2[0, h2].astype(F32)
    acc[...] = rhs[1] - incoming

    @pl.when(two)
    def _():
        loop(0, hi, lambda h2: wait2(1, h2))
        other = p2[1, 0].astype(F32)
        for h2 in range(1, hi):
            other = other + p2[1, h2].astype(F32)
        acc[...] -= other

    ag[1, f] = jnp.where(keep_rows(1), acc[...], 0.0).astype(BF16)
    gather(1, solve(1), weights[2])
    upper = jnp.where(keep_rows(1), acc[...], 0.0)
    xb[...] = upper.astype(BF16)
    weights[3].wait()

    def to_child(c, kid, h2):
        return remote(zs, agb.at[1, f], s_par.at[c, h2], r_gb.at[1, f], (kid, h2 * lo + l))

    def gb_lo(k, q, e, d):
        return remote(agb.at[k, q], agb.at[k, q], s_gb2.at[k, e, d], r_gb.at[k, q], (m, peer(e)))

    def gb_hi(d):
        return remote(agb.at[0, f], agb.at[0, f], s_gb1.at[d], r_gb.at[0, f], (m, near(d) * lo + l))

    def gb_mate(q):
        return remote(agb.at[0, q], agb.at[0, q], s_xb.at[q], r_gb.at[0, q], (mate, f))

    def carry(k, q):
        acct[...] += jnp.dot(agb[k, q], blocks(k, q), preferred_element_type=F32)

    acct[...] = jnp.zeros_like(acct)
    pl.when(top)(lambda: hold(1))

    @pl.when(jnp.logical_not(top))
    def _():
        reduce_lo(up, 1, lifted(1), lambda h2: rs2(1, slot, parent, h2).start(), hi)
        hold(1)

        def from_parent(d):
            q = near(d) * lo + l
            gb_lo(1, q, 0, 0).wait_recv()
            for e in range(1, lo):
                gb_lo(1, q, e, d).start()
            carry(1, q)

        loop(0, hi, from_parent)
        for e in range(1, lo):
            def from_lo(d):
                q = near(d) * lo + (l + lo - e) % lo
                gb_lo(1, q, 0, 0).wait_recv()
                carry(1, q)

            loop(0, hi, from_lo)

    def descend(k):
        ab[...] = jnp.where(keep_columns(k), xs[k] - acct[...], 0.0).astype(BF16)

        def produce(q):
            return jnp.dot(ab[...], columns(k, q), preferred_element_type=F32)

        total = reduce_lo(down, k, produce, lambda h2: rs2b(k, h2).start(), hi - 1, lambda h2: h2 <= h)
        acct[...] = total(h).astype(F32)

        for d in range(1, hi):
            source = near(d)

            @pl.when(source > h)
            def _():
                remote(
                    p2b.at[k, source], p2b.at[k, source], s_b2.at[k, 0], r_b2.at[k, source], (mate, f)
                ).wait_recv()
                acct[...] += p2b[k, source].astype(F32)

        return jnp.where(keep_columns(k), acct[...], 0.0)

    solved = descend(1)
    zs[...] = solved.astype(BF16)

    @pl.when(jnp.logical_not(odd))
    def _():
        loop(0, hi, lambda d: to_child(0, kid0, near(d)).start())

    @pl.when(two)
    def _():
        loop(0, hi, lambda d: to_child(1, kid1, near(d)).start())

    acct[...] = jnp.zeros_like(acct)

    @pl.when(odd)
    def _():
        agb[0, f] = zs[...]
        for d in range(1, hi):
            gb_hi(d).start()
        for e in range(1, lo):
            gb_lo(0, f, e, 0).start()
        gb_mate(f).start()
        carry(0, f)

        def from_hi(d):
            q = near(d) * lo + l
            gb_lo(0, q, 0, 0).wait_recv()
            for e in range(1, lo):
                gb_lo(0, q, e, d).start()
            gb_mate(q).start()
            carry(0, q)

        loop(1, hi, from_hi)
        for e in range(1, lo):
            def from_lo(d):
                q = near(d) * lo + (l + lo - e) % lo
                gb_lo(0, q, 0, 0).wait_recv()
                gb_mate(q).start()
                carry(0, q)

            loop(0, hi, from_lo)

    out[1] = solved.T

    @pl.when(jnp.logical_not(odd))
    def _():
        for e in range(lo):
            def from_mate(d):
                q = near(d) * lo + (l + lo - e) % lo
                gb_lo(0, q, 0, 0).wait_recv()
                carry(0, q)

            loop(0, hi, from_mate)

    out[0] = descend(0).T

    for k in range(2):
        gather_sent(k)
        reduce_sent(down, k, lambda h2: h2 <= h)
        for d in range(1, hi):
            pl.when(near(d) < h)(lambda: rs2b(k, near(d)).wait_send())

    @pl.when(jnp.logical_not(top))
    def _():
        reduce_sent(up, 1)
        loop(0, hi, lambda h2: rs2(1, slot, parent, h2).wait_send())
        for e in range(1, lo):
            loop(0, hi, lambda d: gb_lo(1, near(d) * lo + l, e, d).wait_send())

    @pl.when(jnp.logical_not(odd))
    def _():
        loop(0, hi * lo, lambda q: to_mate(q).wait_send())
        loop(0, hi, lambda d: to_child(0, kid0, near(d)).wait_send())

    @pl.when(two)
    def _():
        loop(0, hi, lambda d: to_child(1, kid1, near(d)).wait_send())

    @pl.when(odd)
    def _():
        reduce_sent(up, 0)
        loop(1, hi, lambda d: rs2(0, 0, m, (h + d) % hi).wait_send())
        for d in range(1, hi):
            gb_hi(d).wait_send()
        for e in range(1, lo):
            loop(0, hi, lambda d: gb_lo(0, near(d) * lo + l, e, d).wait_send())
        loop(0, hi * lo, lambda q: gb_mate(q).wait_send())


def per_device(hi, lo, factor_inverse, contribution, block_map, sep_size, right_side):
    groups = lax.axis_size("sub")
    rows, n = right_side.shape[2:]
    sep_rows = contribution.shape[2]
    count = block_map.shape[2]
    fronts = hi * lo
    steps = jnp.arange(count, dtype=jnp.int32)
    inverse = jnp.sum(
        jnp.where(block_map[0][:, :, None] == steps[None, None, :], steps[None, :, None], 0), axis=1
    )
    dma = pltpu.SemaphoreType.DMA
    vmem = pl.BlockSpec(memory_space=pltpu.VMEM)
    smem = pl.BlockSpec(memory_space=pltpu.SMEM)
    hbm = pl.BlockSpec(memory_space=pl.ANY)
    out = pl.pallas_call(
        functools.partial(kernel, groups, hi, lo),
        out_shape=jax.ShapeDtypeStruct((2, rows, n), F32),
        in_specs=[smem, smem, vmem, hbm, hbm],
        out_specs=vmem,
        scratch_shapes=[
            pltpu.VMEM((2, rows, sep_rows), BF16),
            pltpu.VMEM((count, sep_rows // count, rows), BF16),
            pltpu.VMEM((count, sep_rows // count, rows), BF16),
            pltpu.VMEM((2, fronts, rows, n), BF16),
            pltpu.VMEM((2, fronts, n, rows), BF16),
            pltpu.VMEM((2, fronts, rows, n), BF16),
            pltpu.VMEM((2, fronts, n, rows), BF16),
            pltpu.VMEM((2, lo, hi, rows, n), BF16),
            pltpu.VMEM((2, lo, hi, n, rows), BF16),
            pltpu.VMEM((2, hi, rows, n), BF16),
            pltpu.VMEM((2, hi, n, rows), BF16),
            pltpu.VMEM((fronts, rows, n), BF16),
            pltpu.VMEM((rows, n), BF16),
            pltpu.VMEM((n, rows), BF16),
            pltpu.VMEM((n, rows), BF16),
            pltpu.VMEM((rows, n), F32),
            pltpu.VMEM((2, n, rows), F32),
            pltpu.VMEM((n, rows), F32),
            dma((4,)),
            dma((2, hi)), dma((2, lo, hi)), dma((2, fronts)),
            dma((2, lo, hi)), dma((2, lo, hi)),
            dma((2, hi)), dma((2, hi)),
            dma((fronts,)), dma((fronts,)),
            dma((2, lo, hi)), dma((2, lo, hi)),
            dma((2, hi)), dma((2, hi)),
            dma((2, hi)), dma((hi,)), dma((2, lo, hi)), dma((2, fronts)), dma((fronts,)),
        ],
        compiler_params=pltpu.CompilerParams(
            collective_id=0, has_side_effects=True, vmem_limit_bytes=56 * 1024 * 1024
        ),
    )(
        sep_size,
        inverse,
        right_side[0],
        factor_inverse[0],
        contribution[0].reshape(2, count, sep_rows // count, rows),
    )
    return out[None]


def solution(mesh):
    fronts = mesh.shape["front"]
    hi = min(4, fronts)
    placed = (
        P("sub", None, "front", None),
        P("sub", None, None, "front"),
        P("sub", None, None),
        P("sub", None),
        P("sub", None, "front", None),
    )
    return jax.shard_map(
        functools.partial(per_device, hi, fronts // hi),
        mesh=mesh,
        in_specs=placed,
        out_specs=P("sub", None, "front", None),
        check_vma=False,
    )
```
